128 devices in a mesh: dp: 16 (over z, x_hi, core), ctx: 8 (over y, x_lo).
Axes of the slice: x: 4 (x_hi: 2, x_lo: 2; x = x_hi * 2 + x_lo), y: 4, z: 4, core: 2. Of those that a mesh axis runs over, the one named last changes fastest.
Arguments:
- queries: bfloat16 [32768, 2560], P(('dp', 'ctx')), parts along dimension 0, may hold values from -20 to 20
- key_vectors: bfloat16 [32768, 512], P(('dp', 'ctx')), parts along dimension 0, may hold values from -20 to 20
- value_vectors: bfloat16 [32768, 512], P(('dp', 'ctx')), parts along dimension 0, may hold values from -6 to 6
- output_gradient: bfloat16 [32768, 2560], P(('dp', 'ctx')), parts along dimension 0, may hold values from -6 to 6
- tree_mask: int32 [256, 16], P('dp'), parts along dimension 0, may hold values from 0 to 2, as said below
- tile_order: int32 [256], P(('dp', 'ctx')), parts along dimension 0, may hold values from 0 to 15, each once
Outputs:
- query_gradient: bfloat16 [32768, 2560], P(('dp', 'ctx')), parts along dimension 0
- key_gradient: bfloat16 [32768, 512], P(('dp', 'ctx')), parts along dimension 0
- value_gradient: bfloat16 [32768, 512], P(('dp', 'ctx')), parts along dimension 0
The draws below stay inside these ranges and needn't reach their ends.
There are 16 independent parts, one for each index of `dp`. The reference program is written for one: setup_inputs(seed, part) draws one part's arguments, and reference() takes and returns one part's arrays. A program takes and returns all parts, laid end to end along the dimension named above; each array names one. Nothing has to cross between parts.
Inputs may be any that keep to these rules, and one draw needn't show every extreme that they name: `tree_mask`: rows and columns are tiles of 128 tokens in tree order. Entry (i, i) is 2. For j < i the entry is 1 exactly when tile j lies on the path from the root to tile i, where the path of a tile is that of an earlier parent tile plus itself, and tile 1's parent is tile 0. Entries above the diagonal are 0. Stored tile s (rows s * 128 to (s + 1) * 128 - 1 of every token array) holds tree tile tile_order[s]; every tile of the tree appears once.
All inputs are finite; a program needn't handle non-finite values.
Results may differ from the reference program's by a relative error of at most 0.017.
Values may be sent and summed in bfloat16 or wider, within the bound.
No kernel may reach another device: no remote copies, remote signals or barrier semaphores. Data moves between devices by JAX's collectives and lax.ppermute only.
A program may use at most 128 MiB of HBM per device.

```python
import math
import jax
import jax.numpy as jnp
from jax import lax

QUERY_HEADS = 20
KEY_HEADS = 4
HEAD_WIDTH = 128
TILE = 128
QUERIES_PER_KEY = 5
TREE_TOKENS = 2048
NT = 16


def draw_key_vectors(key, part):
    key = jax.random.fold_in(key, 3)
    key_distribution, key_scale = jax.random.split(key, 2)
    simple_sample = jnp.clip(jax.random.normal(key_distribution, (TREE_TOKENS, KEY_HEADS, HEAD_WIDTH), jnp.float32), -3.5, 3.5)
    row_scale = jnp.exp(jax.random.uniform(key_scale, (TREE_TOKENS, 1, 1), jnp.float32, math.log(0.4), math.log(4.0)))
    value_entries = simple_sample * row_scale
    return value_entries.reshape(TREE_TOKENS, KEY_HEADS * HEAD_WIDTH).astype(jnp.bfloat16)


def draw_queries(key, part):
    key = jax.random.fold_in(key, 5)
    key_distribution, key_scale = jax.random.split(key, 2)
    simple_sample = jnp.clip(jax.random.normal(key_distribution, (TREE_TOKENS, KEY_HEADS, QUERIES_PER_KEY, HEAD_WIDTH), jnp.float32), -3.5, 3.5)
    row_scale = jnp.exp(jax.random.uniform(key_scale, (TREE_TOKENS, 1, 1, 1), jnp.float32, math.log(0.3), math.log(3.0)))
    value_entries = simple_sample * row_scale
    return value_entries.reshape(TREE_TOKENS, QUERY_HEADS * HEAD_WIDTH).astype(jnp.bfloat16)


def draw_tree_mask(key, part):
    key = jax.random.fold_in(key, 7)
    key_chain, key_fork = jax.random.split(key, 2)
    tile_index = jnp.arange(NT, dtype=jnp.int32)
    chain_pick = jax.random.randint(key_chain, (NT,), 0, 2)
    fork_pick = jax.random.randint(key_fork, (NT,), 0, jnp.maximum(tile_index, 1))
    prompt = tile_index < max(NT // 8, 2)
    parent = jnp.where(prompt | (chain_pick == 1), tile_index - 1, fork_pick)
    parent = jnp.maximum(parent, 0).astype(jnp.int32)

    def extend(tile_now, ancestry):
        path_row = lax.dynamic_index_in_dim(ancestry, parent[tile_now], 0, keepdims=False)
        path_row = jnp.where(tile_index == tile_now, 2, jnp.minimum(path_row, 1))
        return lax.dynamic_update_index_in_dim(ancestry, path_row.astype(jnp.int32), tile_now, 0)
    return lax.fori_loop(0, NT, extend, jnp.zeros((NT, NT), jnp.int32))


def shard_levels(stream_key, extent, cuts, smallest, largest):
    gain = 1.0
    for axis_at, blocks in cuts:
        draws = jax.random.uniform(jax.random.fold_in(jax.random.fold_in(stream_key, 6), axis_at), (blocks,), jnp.float32, smallest / len(cuts), largest / len(cuts))
        gain = gain * jnp.repeat(jnp.exp(draws), extent[axis_at] // blocks).reshape((-1,) + (1,) * (len(extent) - 1 - axis_at))
    return gain


def noise(rng, extent, scale, bound, cuts=(), kind=jnp.bfloat16):
    drawn = jax.random.normal(rng, extent, jnp.float32) * scale
    if len(cuts) > 0:
        drawn = shard_levels(rng, extent, cuts, -0.22, 0.18) * drawn
    return jnp.clip(drawn, min=-bound, max=bound).astype(kind)


def setup_inputs(seed: int = 0, part: int = 0) -> dict:
    seeds = jax.random.split(jax.random.key(seed), 7)
    part_keys = jax.random.split(jax.random.fold_in(seeds[6], part), 7)
    queries = draw_queries(jax.random.fold_in(jax.random.fold_in(seeds[6], part), 71), part)
    key_vectors = draw_key_vectors(jax.random.fold_in(jax.random.fold_in(seeds[6], part), 71), part)
    value_vectors = noise(part_keys[2], (TREE_TOKENS, KEY_HEADS * HEAD_WIDTH), 1.0, 6.0, ((0, 8),))
    output_gradient = noise(part_keys[3], (TREE_TOKENS, QUERY_HEADS * HEAD_WIDTH), 1.0, 6.0, ((0, 8),))
    tree_mask = draw_tree_mask(jax.random.fold_in(jax.random.fold_in(seeds[6], part), 71), part)
    tile_order = jax.random.permutation(part_keys[5], NT).astype(jnp.int32)
    return {"queries": queries, "key_vectors": key_vectors, "value_vectors": value_vectors, "output_gradient": output_gradient, "tree_mask": tree_mask, "tile_order": tile_order}


def reference(queries, key_vectors, value_vectors, output_gradient, tree_mask, tile_order):
    overall_rows = queries.shape[0]
    inv_root = HEAD_WIDTH ** -0.5
    within = jnp.arange(overall_rows, dtype=jnp.int32) % TILE
    places = jnp.repeat(tile_order, TILE, total_repeat_length=overall_rows) * TILE + within
    tile_ids = places // TILE
    code_grid = tree_mask[tile_ids][:, tile_ids]
    allowed = (code_grid == 1) | ((code_grid == 2) & (places[None, :] <= places[:, None]))
    stacked = jnp.tile(allowed, (QUERIES_PER_KEY, 1))
    query_grouping = queries.reshape(overall_rows, KEY_HEADS, QUERIES_PER_KEY, HEAD_WIDTH).transpose(1, 2, 0, 3).reshape(KEY_HEADS, QUERIES_PER_KEY * overall_rows, HEAD_WIDTH)
    gradient_groups = output_gradient.reshape(overall_rows, KEY_HEADS, QUERIES_PER_KEY, HEAD_WIDTH).transpose(1, 2, 0, 3).reshape(KEY_HEADS, QUERIES_PER_KEY * overall_rows, HEAD_WIDTH)
    key_grouping = key_vectors.reshape(overall_rows, KEY_HEADS, HEAD_WIDTH).transpose(1, 0, 2)
    value_grouping = value_vectors.reshape(overall_rows, KEY_HEADS, HEAD_WIDTH).transpose(1, 0, 2)

    def one_group(pieces):
        query_group, key_group, value_group, grad_group = pieces
        scores = jnp.dot(query_group, key_group.T, preferred_element_type=jnp.float32) * inv_root
        prob_grad = jnp.dot(grad_group, value_group.T, preferred_element_type=jnp.float32)
        row_top = jnp.max(jnp.where(stacked, scores, -jnp.inf), axis=1, keepdims=True)
        mass_sum = jnp.sum(jnp.where(stacked, jnp.exp(scores - row_top), 0.0), axis=1, keepdims=True)
        log_norm = row_top + jnp.log(mass_sum)
        weights = jnp.where(stacked, jnp.exp(scores - log_norm), 0.0)
        row_delta = jnp.sum(weights * prob_grad, axis=1, keepdims=True)
        prob_bf = weights.astype(jnp.bfloat16)
        dscore = (weights * (prob_grad - row_delta)).astype(jnp.bfloat16)
        value_result = jnp.dot(prob_bf.T, grad_group, preferred_element_type=jnp.float32)
        key_result = jnp.dot(dscore.T, query_group, preferred_element_type=jnp.float32) * inv_root
        query_result = jnp.dot(dscore, key_group, preferred_element_type=jnp.float32) * inv_root
        return query_result, key_result, value_result

    query_result, key_result, value_result = lax.map(one_group, (query_grouping, key_grouping, value_grouping, gradient_groups))
    query_gradient = query_result.reshape(KEY_HEADS, QUERIES_PER_KEY, overall_rows, HEAD_WIDTH).transpose(2, 0, 1, 3).reshape(overall_rows, QUERY_HEADS * HEAD_WIDTH)
    key_gradient = key_result.transpose(1, 0, 2).reshape(overall_rows, KEY_HEADS * HEAD_WIDTH)
    value_gradient = value_result.transpose(1, 0, 2).reshape(overall_rows, KEY_HEADS * HEAD_WIDTH)
    return query_gradient.astype(jnp.bfloat16), key_gradient.astype(jnp.bfloat16), value_gradient.astype(jnp.bfloat16)
```

```python
import functools

import jax
import jax.numpy as jnp
from jax import lax
from jax.experimental import pallas as pl
from jax.experimental.pallas import tpu as pltpu
from jax.sharding import PartitionSpec as P

QUERY_HEADS = 20
KEY_HEADS = 4
HEAD_WIDTH = 128
TILE = 128
GROUP = 5
LOG2E = 1.4426950408889634
INV_ROOT = HEAD_WIDTH**-0.5
NEG = -1e30
ROWS = 256
KEY_BLOCKS = 4
KEY_TILES = 16
QUERY_TILES = 4
WIDE = GROUP * TILE
NT_DIMS = (((1,), (1,)), ((), ()))
TN_DIMS = (((0,), (0,)), ((), ()))


def dot(a, b):
    return jnp.dot(a, b, preferred_element_type=jnp.float32)


def kernel(
    ids_ref,
    mask_ref,
    q_own,
    g_own,
    qg_partner,
    kv0,
    kv1,
    kv2,
    kv3,
    dq_own,
    dq_partner,
    out0,
    out1,
    out2,
    out3,
    q_all,
    g_all,
    e_all,
    dp_all,
    top_all,
    dq_acc,
    dk_acc,
    dv_acc,
    k_all,
    v_all,
    list_ref,
):
    blocks = (kv0, kv1, kv2, kv3)
    half = 2 * ROWS
    for b in range(KEY_BLOCKS):
        k_all[b * half : (b + 1) * half, :] = blocks[b][0:half, :]
        v_all[b * half : (b + 1) * half, :] = blocks[b][half : 2 * half, :]
    for t in range(QUERY_TILES):
        for j in range(GROUP):
            to = slice(j * TILE, (j + 1) * TILE)
            if t < 2:
                rows = slice(t * TILE, (t + 1) * TILE)
                q_all[t, to, :] = q_own[rows, to]
                g_all[t, to, :] = g_own[rows, to]
            else:
                rows = slice((t - 2) * TILE, (t - 1) * TILE)
                q_all[t, to, :] = qg_partner[rows, to]
                g_all[t, to, :] = qg_partner[slice(ROWS + (t - 2) * TILE, ROWS + (t - 1) * TILE), to]
    dk_acc[...] = jnp.zeros_like(dk_acc)
    dv_acc[...] = jnp.zeros_like(dv_acc)
    key_row = lax.broadcasted_iota(jnp.int32, (TILE, TILE), 0)
    query_col = lax.broadcasted_iota(jnp.int32, (TILE, TILE), 1)
    causal = key_row <= query_col

    def per_query_tile(t, _):
        my_tile = ids_ref[t]

        def collect(u, count):
            code = mask_ref[my_tile, ids_ref[u]]
            list_ref[count] = u
            return count + jnp.where(code == 1, 1, 0)

        list_ref[0] = t
        odd_end = lax.fori_loop(0, KEY_TILES, collect, 2) - 2
        total = odd_end + 1
        paired = total % 2 == 0
        last = list_ref[odd_end + 1]
        list_ref[1] = jnp.where(paired, last, t)
        rest = jnp.where(paired, odd_end - 1, odd_end)
        chunks = 1 + rest // 2
        q = q_all[t]
        g = g_all[t]

        def tiles_of(c):
            first = pl.multiple_of(list_ref[2 * c] * TILE, TILE)
            second = pl.multiple_of(list_ref[2 * c + 1] * TILE, TILE)
            return first, second

        def rows_of(ref, first, second):
            return jnp.concatenate([ref[pl.ds(first, TILE), :], ref[pl.ds(second, TILE), :]], axis=0)

        def products(c):
            first, second = tiles_of(c)
            k = rows_of(k_all, first, second)
            v = rows_of(v_all, first, second)
            s = lax.dot_general(k, q, NT_DIMS, preferred_element_type=jnp.float32)
            dp = lax.dot_general(v, g, NT_DIMS, preferred_element_type=jnp.float32)
            return s * (INV_ROOT * LOG2E), dp

        s, dp = products(0)
        ok = jnp.concatenate([causal, jnp.broadcast_to(paired, (TILE, TILE))], axis=0)
        s = jnp.where(jnp.concatenate([ok] * GROUP, axis=1), s, NEG)
        top = jnp.max(s, axis=0, keepdims=True)
        e = jnp.exp2(s - top)
        e_all[0] = e
        dp_all[0] = dp
        top_all[0, 0:1, :] = top
        mass = jnp.sum(e, axis=0, keepdims=True)
        weighted = jnp.sum(e * dp, axis=0, keepdims=True)

        def forward(c, carry):
            top, mass, weighted = carry
            s, dp = products(c)
            new_top = jnp.maximum(top, jnp.max(s, axis=0, keepdims=True))
            e = jnp.exp2(s - new_top)
            e_all[c] = e
            dp_all[c] = dp
            top_all[c, 0:1, :] = new_top
            shrink = jnp.exp2(top - new_top)
            return (
                new_top,
                mass * shrink + jnp.sum(e, axis=0, keepdims=True),
                weighted * shrink + jnp.sum(e * dp, axis=0, keepdims=True),
            )

        top, mass, weighted = lax.fori_loop(1, chunks, forward, (top, mass, weighted))
        inv_mass = 1.0 / mass
        delta = weighted * inv_mass
        dq_acc[...] = jnp.zeros_like(dq_acc)

        def backward(c, _):
            first, second = tiles_of(c)
            factor = jnp.exp2(top_all[c, 0:1, :] - top) * inv_mass
            p = e_all[c] * factor
            ds = p * (dp_all[c] - delta)
            p = p.astype(jnp.bfloat16)
            ds = ds.astype(jnp.bfloat16)
            dv = dot(p, g)
            dk = dot(ds, q)
            k = rows_of(k_all, first, second)
            dq_acc[...] += lax.dot_general(ds, k, TN_DIMS, preferred_element_type=jnp.float32)
            dv_acc[pl.ds(first, TILE), :] += dv[:TILE]
            dk_acc[pl.ds(first, TILE), :] += dk[:TILE]
            dv_acc[pl.ds(second, TILE), :] += dv[TILE:]
            dk_acc[pl.ds(second, TILE), :] += dk[TILE:]
            return 0

        lax.fori_loop(0, chunks, backward, 0)
        dq = (dq_acc[...] * INV_ROOT).astype(jnp.bfloat16)

        @pl.when(t < 2)
        def _():
            rows = pl.ds(pl.multiple_of(t * TILE, TILE), TILE)
            for j in range(GROUP):
                to = slice(j * TILE, (j + 1) * TILE)
                dq_own[rows, to] = dq[to, :]

        @pl.when(t >= 2)
        def _():
            rows = pl.ds(pl.multiple_of((t - 2) * TILE, TILE), TILE)
            for j in range(GROUP):
                to = slice(j * TILE, (j + 1) * TILE)
                dq_partner[rows, to] = dq[to, :]

        return 0

    lax.fori_loop(0, QUERY_TILES, per_query_tile, 0)
    for b, out in enumerate((out0, out1, out2, out3)):
        rows = slice(b * half, (b + 1) * half)
        out[0:half, :] = dk_acc[rows, :].astype(out.dtype)
        out[half : 2 * half, :] = dv_acc[rows, :].astype(out.dtype)


def head_backward(ids, mask, q_own, g_own, qg_partner, blocks):
    vmem = pl.BlockSpec(memory_space=pltpu.VMEM)
    smem = pl.BlockSpec(memory_space=pltpu.SMEM)
    flops = 8 * 10 * 2 * QUERY_TILES * TILE * TILE * WIDE
    return pl.pallas_call(
        kernel,
        out_shape=(
            jax.ShapeDtypeStruct((ROWS, WIDE), jnp.bfloat16),
            jax.ShapeDtypeStruct((ROWS, WIDE), jnp.bfloat16),
            jax.ShapeDtypeStruct((4 * ROWS, HEAD_WIDTH), jnp.float32),
            jax.ShapeDtypeStruct((4 * ROWS, HEAD_WIDTH), jnp.bfloat16),
            jax.ShapeDtypeStruct((4 * ROWS, HEAD_WIDTH), jnp.bfloat16),
            jax.ShapeDtypeStruct((4 * ROWS, HEAD_WIDTH), jnp.bfloat16),
        ),
        in_specs=[smem, smem] + [vmem] * 7,
        out_specs=(vmem,) * 6,
        scratch_shapes=[
            pltpu.VMEM((QUERY_TILES, WIDE, HEAD_WIDTH), jnp.bfloat16),
            pltpu.VMEM((QUERY_TILES, WIDE, HEAD_WIDTH), jnp.bfloat16),
            pltpu.VMEM((KEY_TILES // 2, 2 * TILE, WIDE), jnp.float32),
            pltpu.VMEM((KEY_TILES // 2, 2 * TILE, WIDE), jnp.float32),
            pltpu.VMEM((KEY_TILES // 2, 8, WIDE), jnp.float32),
            pltpu.VMEM((WIDE, HEAD_WIDTH), jnp.float32),
            pltpu.VMEM((KEY_TILES * TILE, HEAD_WIDTH), jnp.float32),
            pltpu.VMEM((KEY_TILES * TILE, HEAD_WIDTH), jnp.float32),
            pltpu.VMEM((KEY_TILES * TILE, HEAD_WIDTH), jnp.bfloat16),
            pltpu.VMEM((KEY_TILES * TILE, HEAD_WIDTH), jnp.bfloat16),
            pltpu.SMEM((KEY_TILES + 4,), jnp.int32),
        ],
        compiler_params=pltpu.CompilerParams(vmem_limit_bytes=40 * 1024 * 1024),
        cost_estimate=pl.CostEstimate(flops=flops, bytes_accessed=6_000_000, transcendentals=0),
    )(ids, mask, q_own, g_own, qg_partner, *blocks)


def ring_pairs(dy, dx):
    pairs = []
    for c in range(8):
        y, x = divmod(c, 2)
        pairs.append((c, ((y + dy) % 4) * 2 + (x + dx) % 2))
    return pairs


def move(value, dy, dx):
    return lax.ppermute(value, "ctx", ring_pairs(dy, dx))


def local(queries, key_vectors, value_vectors, output_gradient, tree_mask, tile_order):
    x = lax.axis_index("ctx") % 2

    def columns(array, side, head, width):
        return lax.dynamic_slice_in_dim(array, (2 * side + head) * width, width, axis=1)

    ids_row = jnp.pad(tile_order.astype(jnp.bfloat16), (0, HEAD_WIDTH - 2))
    ids_rows = jnp.broadcast_to(ids_row[None, :], (16, HEAD_WIDTH))
    sent = jnp.concatenate(
        [columns(a, 1 - x, h, HEAD_WIDTH) for h in range(2) for a in (key_vectors, value_vectors)]
        + [ids_rows],
        axis=0,
    )
    got = move(sent, 0, 1)
    partner_ids = got[4 * ROWS : 4 * ROWS + 16]
    both_ids = ids_rows + jnp.roll(partner_ids, 2, axis=1)

    partner_qg = [
        move(
            jnp.concatenate(
                [
                    columns(queries, 1 - x, h, WIDE),
                    columns(output_gradient, 1 - x, h, WIDE),
                ],
                axis=0,
            ),
            0,
            1,
        )
        for h in range(2)
    ]
    steps = (1, -1, 2)
    query_own, query_back, home = [], [], []
    ids = None
    for h in range(2):
        mine = jnp.concatenate(
            [
                columns(key_vectors, x, h, HEAD_WIDTH),
                got[2 * h * ROWS : (2 * h + 1) * ROWS],
                columns(value_vectors, x, h, HEAD_WIDTH),
                got[(2 * h + 1) * ROWS : (2 * h + 2) * ROWS],
                both_ids,
            ],
            axis=0,
        )
        arrived = [move(mine, s, 0) for s in steps]
        if ids is None:
            ids = jnp.concatenate([b[4 * ROWS, 0:4] for b in [mine] + arrived]).astype(jnp.int32)
        outs = head_backward(
            ids,
            tree_mask,
            columns(queries, x, h, WIDE),
            columns(output_gradient, x, h, WIDE),
            partner_qg[h],
            [mine] + arrived,
        )
        query_own.append(outs[0])
        query_back.append(move(outs[1], 0, 1))
        total = outs[2]
        for s, part in zip(steps, outs[3:]):
            total = total + move(part, -s, 0).astype(jnp.float32)
        away = jnp.concatenate([total[ROWS : 2 * ROWS], total[3 * ROWS : 4 * ROWS]], axis=0)
        back = move(away.astype(jnp.bfloat16), 0, 1).astype(jnp.float32)
        home.append((total[0:ROWS], total[2 * ROWS : 3 * ROWS], back[0:ROWS], back[ROWS:]))
    first = x == 0

    def arrange(own, other):
        low = [jnp.where(first, a, b) for a, b in zip(own, other)]
        high = [jnp.where(first, b, a) for a, b in zip(own, other)]
        return jnp.concatenate(low + high, axis=1)

    query_gradient = arrange(query_own, query_back)
    key_gradient = arrange([h[0] for h in home], [h[2] for h in home]) * INV_ROOT
    value_gradient = arrange([h[1] for h in home], [h[3] for h in home])
    return query_gradient, key_gradient.astype(jnp.bfloat16), value_gradient.astype(jnp.bfloat16)


def solution(mesh):
    placed = (
        P(("dp", "ctx"), None),
        P(("dp", "ctx"), None),
        P(("dp", "ctx"), None),
        P(("dp", "ctx"), None),
        P("dp", None),
        P(("dp", "ctx")),
    )
    return jax.shard_map(
        local,
        mesh=mesh,
        in_specs=placed,
        out_specs=(P(("dp", "ctx"), None), P(("dp", "ctx"), None), P(("dp", "ctx"), None)),
        check_vma=False,
    )
```

```python
import functools

import jax
import jax.numpy as jnp
from jax import lax
from jax.experimental import pallas as pl
from jax.experimental.pallas import tpu as pltpu
from jax.sharding import PartitionSpec as P

QUERY_HEADS = 20
KEY_HEADS = 4
HEAD_WIDTH = 128
TILE = 128
GROUP = 5
LOG2E = 1.4426950408889634
INV_ROOT = HEAD_WIDTH**-0.5
NEG = -1e30
ROWS = 256
KEY_BLOCKS = 4
KEY_TILES = 16
QUERY_TILES = 4
WIDE = GROUP * TILE
NT_DIMS = (((1,), (1,)), ((), ()))
TN_DIMS = (((0,), (0,)), ((), ()))


def dot(a, b):
    return jnp.dot(a, b, preferred_element_type=jnp.float32)


def kernel(
    ids_ref,
    mask_ref,
    q_own,
    g_own,
    qg_partner,
    kv0,
    kv1,
    kv2,
    kv3,
    dq_own,
    dq_partner,
    out0,
    out1,
    out2,
    out3,
    q_all,
    g_all,
    e_all,
    dp_all,
    top_all,
    e_first,
    dp_first,
    stats,
    dq_all,
    dk_acc,
    dv_acc,
    k_all,
    v_all,
    list_ref,
    count_ref,
):
    blocks = (kv0, kv1, kv2, kv3)
    half = 2 * ROWS
    for b in range(KEY_BLOCKS):
        k_all[b * half : (b + 1) * half, :] = blocks[b][0:half, :]
        v_all[b * half : (b + 1) * half, :] = blocks[b][half : 2 * half, :]
    for t in range(QUERY_TILES):
        for j in range(GROUP):
            to = slice(j * TILE, (j + 1) * TILE)
            if t < 2:
                rows = slice(t * TILE, (t + 1) * TILE)
                q_all[t, to, :] = q_own[rows, to]
                g_all[t, to, :] = g_own[rows, to]
            else:
                rows = slice((t - 2) * TILE, (t - 1) * TILE)
                q_all[t, to, :] = qg_partner[rows, to]
                g_all[t, to, :] = qg_partner[slice(ROWS + (t - 2) * TILE, ROWS + (t - 1) * TILE), to]
    dk_acc[...] = jnp.zeros_like(dk_acc)
    dv_acc[...] = jnp.zeros_like(dv_acc)
    key_row = lax.broadcasted_iota(jnp.int32, (TILE, TILE), 0)
    query_col = lax.broadcasted_iota(jnp.int32, (TILE, TILE), 1)
    causal = key_row <= query_col

    evens, counts = [], []
    for t in range(QUERY_TILES):
        my_tile = ids_ref[t]

        def collect(u, count, t=t, my_tile=my_tile):
            list_ref[t, count] = u
            return count + jnp.where(mask_ref[my_tile, ids_ref[u]] == 1, 1, 0)

        ancestors = lax.fori_loop(0, KEY_TILES, collect, 2) - 2
        even = ancestors % 2 == 1
        last = list_ref[t, ancestors + 1]
        list_ref[t, 0] = t
        list_ref[t, 1] = jnp.where(even, last, t)
        chunks = 1 + ancestors // 2
        count_ref[t] = chunks
        evens.append(even)

    def tiles_of(t, c):
        first = pl.multiple_of(list_ref[t, 2 * c] * TILE, TILE)
        second = pl.multiple_of(list_ref[t, 2 * c + 1] * TILE, TILE)
        return first, second

    def rows_of(ref, tiles):
        return jnp.concatenate([ref[pl.ds(i, TILE), :] for i in tiles], axis=0)

    def products(t, c):
        tiles = tiles_of(t, c)
        s = lax.dot_general(rows_of(k_all, tiles), q_all[t], NT_DIMS, preferred_element_type=jnp.float32)
        dp = lax.dot_general(rows_of(v_all, tiles), g_all[t], NT_DIMS, preferred_element_type=jnp.float32)
        return s * (INV_ROOT * LOG2E), dp

    def spread(t, c, e, dp, factor, delta):
        first, second = tiles_of(t, c)
        p = e * factor
        ds = (p * (dp - delta)).astype(jnp.bfloat16)
        p = p.astype(jnp.bfloat16)
        dv = dot(p, g_all[t])
        dk = dot(ds, q_all[t])
        dv_acc[pl.ds(first, TILE), :] += dv[:TILE]
        dk_acc[pl.ds(first, TILE), :] += dk[:TILE]
        dv_acc[pl.ds(second, TILE), :] += dv[TILE:]
        dk_acc[pl.ds(second, TILE), :] += dk[TILE:]
        return lax.dot_general(ds, rows_of(k_all, (first, second)), TN_DIMS, preferred_element_type=jnp.float32)

    for t in range(QUERY_TILES):
        s, dp = products(t, 0)
        ok = jnp.concatenate([causal, jnp.broadcast_to(evens[t], (TILE, TILE))], axis=0)
        s = jnp.where(jnp.concatenate([ok] * GROUP, axis=1), s, NEG)
        top = jnp.max(s, axis=0, keepdims=True)
        e = jnp.exp2(s - top)
        e_first[t] = e
        dp_first[t] = dp
        stats[t, 0:1, :] = top
        stats[t, 1:2, :] = jnp.sum(e, axis=0, keepdims=True)
        stats[t, 2:3, :] = jnp.sum(e * dp, axis=0, keepdims=True)

    def per_query_tile(t, _):
        chunks = count_ref[t]

        def forward(c, carry):
            top, mass, weighted = carry
            s, dp = products(t, c)
            new_top = jnp.maximum(top, jnp.max(s, axis=0, keepdims=True))
            e = jnp.exp2(s - new_top)
            e_all[c] = e
            dp_all[c] = dp
            top_all[c, 0:1, :] = new_top
            shrink = jnp.exp2(top - new_top)
            return (
                new_top,
                mass * shrink + jnp.sum(e, axis=0, keepdims=True),
                weighted * shrink + jnp.sum(e * dp, axis=0, keepdims=True),
            )

        top = stats[t, 0:1, :]
        carry = (top, stats[t, 1:2, :], stats[t, 2:3, :])
        pairs = (chunks - 1) // 2
        carry = lax.fori_loop(0, pairs, lambda i, carry: forward(2 * i + 2, forward(2 * i + 1, carry)), carry)
        final, mass, weighted = lax.fori_loop(1 + 2 * pairs, chunks, forward, carry)
        inv_mass = 1.0 / mass
        delta = weighted * inv_mass
        stats[t, 3:4, :] = jnp.exp2(top - final) * inv_mass
        stats[t, 4:5, :] = delta
        dq_all[t] = jnp.zeros((WIDE, HEAD_WIDTH), jnp.float32)

        def backward(c, _):
            factor = jnp.exp2(top_all[c, 0:1, :] - final) * inv_mass
            dq_all[t] += spread(t, c, e_all[c], dp_all[c], factor, delta)
            return 0

        lax.fori_loop(0, pairs, lambda i, _: backward(2 * i + 2, backward(2 * i + 1, 0)), 0)
        lax.fori_loop(1 + 2 * pairs, chunks, backward, 0)
        return 0

    lax.fori_loop(0, QUERY_TILES, per_query_tile, 0)
    for t in range(QUERY_TILES):
        dq = dq_all[t] + spread(t, 0, e_first[t], dp_first[t], stats[t, 3:4, :], stats[t, 4:5, :])
        dq = (dq * INV_ROOT).astype(jnp.bfloat16)
        out = dq_own if t < 2 else dq_partner
        rows = slice((t % 2) * TILE, (t % 2 + 1) * TILE)
        for j in range(GROUP):
            out[rows, j * TILE : (j + 1) * TILE] = dq[j * TILE : (j + 1) * TILE, :]
    for b, out in enumerate((out0, out1, out2, out3)):
        rows = slice(b * half, (b + 1) * half)
        out[0:half, :] = dk_acc[rows, :].astype(out.dtype)
        out[half : 2 * half, :] = dv_acc[rows, :].astype(out.dtype)


def head_backward(ids, mask, q_own, g_own, qg_partner, blocks):
    vmem = pl.BlockSpec(memory_space=pltpu.VMEM)
    smem = pl.BlockSpec(memory_space=pltpu.SMEM)
    flops = 8 * 10 * 2 * QUERY_TILES * TILE * TILE * WIDE
    return pl.pallas_call(
        kernel,
        out_shape=(
            jax.ShapeDtypeStruct((ROWS, WIDE), jnp.bfloat16),
            jax.ShapeDtypeStruct((ROWS, WIDE), jnp.bfloat16),
            jax.ShapeDtypeStruct((4 * ROWS, HEAD_WIDTH), jnp.float32),
            jax.ShapeDtypeStruct((4 * ROWS, HEAD_WIDTH), jnp.bfloat16),
            jax.ShapeDtypeStruct((4 * ROWS, HEAD_WIDTH), jnp.bfloat16),
            jax.ShapeDtypeStruct((4 * ROWS, HEAD_WIDTH), jnp.bfloat16),
        ),
        in_specs=[smem, smem] + [vmem] * 7,
        out_specs=(vmem,) * 6,
        scratch_shapes=[
            pltpu.VMEM((QUERY_TILES, WIDE, HEAD_WIDTH), jnp.bfloat16),
            pltpu.VMEM((QUERY_TILES, WIDE, HEAD_WIDTH), jnp.bfloat16),
            pltpu.VMEM((KEY_TILES // 2, 2 * TILE, WIDE), jnp.float32),
            pltpu.VMEM((KEY_TILES // 2, 2 * TILE, WIDE), jnp.float32),
            pltpu.VMEM((KEY_TILES // 2, 8, WIDE), jnp.float32),
            pltpu.VMEM((QUERY_TILES, 2 * TILE, WIDE), jnp.float32),
            pltpu.VMEM((QUERY_TILES, 2 * TILE, WIDE), jnp.float32),
            pltpu.VMEM((QUERY_TILES, 8, WIDE), jnp.float32),
            pltpu.VMEM((QUERY_TILES, WIDE, HEAD_WIDTH), jnp.float32),
            pltpu.VMEM((KEY_TILES * TILE, HEAD_WIDTH), jnp.float32),
            pltpu.VMEM((KEY_TILES * TILE, HEAD_WIDTH), jnp.float32),
            pltpu.VMEM((KEY_TILES * TILE, HEAD_WIDTH), jnp.bfloat16),
            pltpu.VMEM((KEY_TILES * TILE, HEAD_WIDTH), jnp.bfloat16),
            pltpu.SMEM((QUERY_TILES, KEY_TILES + 4), jnp.int32),
            pltpu.SMEM((QUERY_TILES,), jnp.int32),
        ],
        compiler_params=pltpu.CompilerParams(vmem_limit_bytes=32 * 1024 * 1024),
        cost_estimate=pl.CostEstimate(flops=flops, bytes_accessed=6_000_000, transcendentals=0),
    )(ids, mask, q_own, g_own, qg_partner, *blocks)


def ring_pairs(dy, dx):
    pairs = []
    for c in range(8):
        y, x = divmod(c, 2)
        pairs.append((c, ((y + dy) % 4) * 2 + (x + dx) % 2))
    return pairs


def move(value, dy, dx):
    return lax.ppermute(value, "ctx", ring_pairs(dy, dx))


def local(queries, key_vectors, value_vectors, output_gradient, tree_mask, tile_order):
    x = lax.axis_index("ctx") % 2

    def columns(array, side, head, width):
        return lax.dynamic_slice_in_dim(array, (2 * side + head) * width, width, axis=1)

    both_wide = 2 * HEAD_WIDTH
    ids_row = jnp.pad(tile_order.astype(jnp.bfloat16), (0, both_wide - 2))
    ids_rows = jnp.broadcast_to(ids_row[None, :], (16, both_wide))
    sent = jnp.concatenate(
        [
            lax.dynamic_slice_in_dim(a, (1 - x) * both_wide, both_wide, axis=1)
            for a in (key_vectors, value_vectors)
        ]
        + [ids_rows],
        axis=0,
    )
    got = move(sent, 0, 1)
    both_ids = ids_rows[:, :HEAD_WIDTH] + jnp.roll(got[2 * ROWS :, :HEAD_WIDTH], 2, axis=1)

    partner_qg = [
        move(
            jnp.concatenate(
                [
                    columns(queries, 1 - x, h, WIDE),
                    columns(output_gradient, 1 - x, h, WIDE),
                ],
                axis=0,
            ),
            0,
            1,
        )
        for h in range(2)
    ]
    steps = (1, -1, 2)
    query_own, query_back, home = [], [], []
    ids = None
    for h in range(2):
        mine = jnp.concatenate(
            [
                columns(key_vectors, x, h, HEAD_WIDTH),
                got[0:ROWS, h * HEAD_WIDTH : (h + 1) * HEAD_WIDTH],
                columns(value_vectors, x, h, HEAD_WIDTH),
                got[ROWS : 2 * ROWS, h * HEAD_WIDTH : (h + 1) * HEAD_WIDTH],
                both_ids,
            ],
            axis=0,
        )
        arrived = [move(mine, s, 0) for s in steps]
        if ids is None:
            ids = jnp.concatenate([b[4 * ROWS, 0:4] for b in [mine] + arrived]).astype(jnp.int32)
        outs = head_backward(
            ids,
            tree_mask,
            columns(queries, x, h, WIDE),
            columns(output_gradient, x, h, WIDE),
            partner_qg[h],
            [mine] + arrived,
        )
        if h == 1:
            parts, query_back[0] = lax.optimization_barrier((outs[1:], query_back[0]))
            outs = (outs[0],) + tuple(parts)
        query_own.append(outs[0])
        query_back.append(move(outs[1], 0, 1))
        total = outs[2]
        for s, part in zip(steps, outs[3:]):
            total = total + move(part, -s, 0).astype(jnp.float32)
        away = jnp.concatenate([total[ROWS : 2 * ROWS], total[3 * ROWS : 4 * ROWS]], axis=0)
        back = move(away.astype(jnp.bfloat16), 0, 1).astype(jnp.float32)
        home.append((total[0:ROWS], total[2 * ROWS : 3 * ROWS], back[0:ROWS], back[ROWS:]))
    first = x == 0

    def arrange(own, other):
        low = [jnp.where(first, a, b) for a, b in zip(own, other)]
        high = [jnp.where(first, b, a) for a, b in zip(own, other)]
        return jnp.concatenate(low + high, axis=1)

    query_gradient = arrange(query_own, query_back)
    key_gradient = arrange([h[0] for h in home], [h[2] for h in home]) * INV_ROOT
    value_gradient = arrange([h[1] for h in home], [h[3] for h in home])
    return query_gradient, key_gradient.astype(jnp.bfloat16), value_gradient.astype(jnp.bfloat16)


def solution(mesh):
    placed = (
        P(("dp", "ctx"), None),
        P(("dp", "ctx"), None),
        P(("dp", "ctx"), None),
        P(("dp", "ctx"), None),
        P("dp", None),
        P(("dp", "ctx")),
    )
    return jax.shard_map(
        local,
        mesh=mesh,
        in_specs=placed,
        out_specs=(P(("dp", "ctx"), None), P(("dp", "ctx"), None), P(("dp", "ctx"), None)),
        check_vma=False,
    )
```

```python
import functools

import jax
import jax.numpy as jnp
from jax import lax
from jax.experimental import pallas as pl
from jax.experimental.pallas import tpu as pltpu
from jax.sharding import PartitionSpec as P

QUERY_HEADS = 20
KEY_HEADS = 4
HEAD_WIDTH = 128
TILE = 128
GROUP = 5
LOG2E = 1.4426950408889634
INV_ROOT = HEAD_WIDTH**-0.5
NEG = -1e30
ROWS = 256
KEY_BLOCKS = 4
KEY_TILES = 16
QUERY_TILES = 4
WIDE = GROUP * TILE
NT_DIMS = (((1,), (1,)), ((), ()))
TN_DIMS = (((0,), (0,)), ((), ()))


def dot(a, b):
    return jnp.dot(a, b, preferred_element_type=jnp.float32)


def kernel(
    ids_ref,
    mask_ref,
    q_own,
    g_own,
    qg_partner,
    kv0,
    kv1,
    kv2,
    kv3,
    dq_own,
    dq_partner,
    out0,
    out1,
    out2,
    out3,
    q_all,
    g_all,
    e_all,
    dp_all,
    top_all,
    e_first,
    dp_first,
    stats,
    dq_all,
    dk_acc,
    dv_acc,
    k_all,
    v_all,
    list_ref,
    count_ref,
):
    blocks = (kv0, kv1, kv2, kv3)
    half = 2 * ROWS
    for b in range(KEY_BLOCKS):
        k_all[b * half : (b + 1) * half, :] = blocks[b][0:half, :]
        v_all[b * half : (b + 1) * half, :] = blocks[b][half : 2 * half, :]
    for t in range(QUERY_TILES):
        for j in range(GROUP):
            to = slice(j * TILE, (j + 1) * TILE)
            if t < 2:
                rows = slice(t * TILE, (t + 1) * TILE)
                q_all[t, to, :] = q_own[rows, to]
                g_all[t, to, :] = g_own[rows, to]
            else:
                rows = slice((t - 2) * TILE, (t - 1) * TILE)
                q_all[t, to, :] = qg_partner[rows, to]
                g_all[t, to, :] = qg_partner[slice(ROWS + (t - 2) * TILE, ROWS + (t - 1) * TILE), to]
    key_row = lax.broadcasted_iota(jnp.int32, (TILE, TILE), 0)
    query_col = lax.broadcasted_iota(jnp.int32, (TILE, TILE), 1)
    causal = key_row <= query_col

    evens, counts = [], []
    for t in range(QUERY_TILES):
        my_tile = ids_ref[t]

        def collect(u, count, t=t, my_tile=my_tile):
            list_ref[t, count] = u
            return count + jnp.where(mask_ref[my_tile, ids_ref[u]] == 1, 1, 0)

        ancestors = lax.fori_loop(0, KEY_TILES, collect, 2) - 2
        even = ancestors % 2 == 1
        last = list_ref[t, ancestors + 1]
        list_ref[t, 0] = t
        list_ref[t, 1] = jnp.where(even, last, t)
        chunks = 1 + ancestors // 2
        count_ref[t] = chunks
        evens.append(even)

    def tiles_of(t, c):
        first = pl.multiple_of(list_ref[t, 2 * c] * TILE, TILE)
        second = pl.multiple_of(list_ref[t, 2 * c + 1] * TILE, TILE)
        return first, second

    def rows_of(ref, tiles):
        return jnp.concatenate([ref[pl.ds(i, TILE), :] for i in tiles], axis=0)

    def products(t, c):
        tiles = tiles_of(t, c)
        s = lax.dot_general(rows_of(k_all, tiles), q_all[t], NT_DIMS, preferred_element_type=jnp.float32)
        dp = lax.dot_general(rows_of(v_all, tiles), g_all[t], NT_DIMS, preferred_element_type=jnp.float32)
        return s * (INV_ROOT * LOG2E), dp

    def spread(t, c, e, dp, factor, delta):
        first, second = tiles_of(t, c)
        p = e * factor
        ds = (p * (dp - delta)).astype(jnp.bfloat16)
        p = p.astype(jnp.bfloat16)
        dv = dot(p, g_all[t])
        dk = dot(ds, q_all[t])
        dv_acc[pl.ds(first, TILE), :] += dv[:TILE]
        dk_acc[pl.ds(first, TILE), :] += dk[:TILE]
        dv_acc[pl.ds(second, TILE), :] += dv[TILE:]
        dk_acc[pl.ds(second, TILE), :] += dk[TILE:]
        return ds, rows_of(k_all, (first, second))

    def gather_dq(ds, k):
        return lax.dot_general(ds, k, TN_DIMS, preferred_element_type=jnp.float32)

    for t in range(QUERY_TILES):
        s, dp = products(t, 0)
        for sums in (dk_acc, dv_acc):
            sums[t * half : (t + 1) * half, :] = jnp.zeros((half, HEAD_WIDTH), jnp.float32)
        ok = jnp.concatenate([causal, jnp.broadcast_to(evens[t], (TILE, TILE))], axis=0)
        s = jnp.where(jnp.concatenate([ok] * GROUP, axis=1), s, NEG)
        top = jnp.max(s, axis=0, keepdims=True)
        e = jnp.exp2(s - top)
        e_first[t] = e
        dp_first[t] = dp
        stats[t, 0:1, :] = top
        stats[t, 1:2, :] = jnp.sum(e, axis=0, keepdims=True)
        stats[t, 2:3, :] = jnp.sum(e * dp, axis=0, keepdims=True)

    def per_query_tile(t, _):
        chunks = count_ref[t]

        def forward(c, carry):
            top, mass, weighted = carry
            s, dp = products(t, c)
            new_top = jnp.maximum(top, jnp.max(s, axis=0, keepdims=True))
            e = jnp.exp2(s - new_top)
            e_all[c - 1] = e
            dp_all[c - 1] = dp
            top_all[c - 1, 0:1, :] = new_top
            shrink = jnp.exp2(top - new_top)
            return (
                new_top,
                mass * shrink + jnp.sum(e, axis=0, keepdims=True),
                weighted * shrink + jnp.sum(e * dp, axis=0, keepdims=True),
            )

        top = stats[t, 0:1, :]
        carry = (top, stats[t, 1:2, :], stats[t, 2:3, :])
        pairs = (chunks - 1) // 2
        carry = lax.fori_loop(0, pairs, lambda i, carry: forward(2 * i + 2, forward(2 * i + 1, carry)), carry)
        final, mass, weighted = lax.fori_loop(1 + 2 * pairs, chunks, forward, carry)
        inv_mass = 1.0 / mass
        delta = weighted * inv_mass
        stats[t, 3:4, :] = jnp.exp2(top - final) * inv_mass
        stats[t, 4:5, :] = delta
        dq_all[t] = jnp.zeros((WIDE, HEAD_WIDTH), jnp.float32)

        def backward(c):
            factor = jnp.exp2(top_all[c - 1, 0:1, :] - final) * inv_mass
            return spread(t, c, e_all[c - 1], dp_all[c - 1], factor, delta)

        def backward_two(i, _):
            ds0, k0 = backward(2 * i + 1)
            ds1, k1 = backward(2 * i + 2)
            dq_all[t] += gather_dq(jnp.concatenate([ds0, ds1], axis=0), jnp.concatenate([k0, k1], axis=0))
            return 0

        def backward_one(c, _):
            dq_all[t] += gather_dq(*backward(c))
            return 0

        lax.fori_loop(0, pairs, backward_two, 0)
        lax.fori_loop(1 + 2 * pairs, chunks, backward_one, 0)
        return 0

    lax.fori_loop(0, QUERY_TILES, per_query_tile, 0)
    for t in range(QUERY_TILES):
        dq = dq_all[t] + gather_dq(*spread(t, 0, e_first[t], dp_first[t], stats[t, 3:4, :], stats[t, 4:5, :]))
        dq = (dq * INV_ROOT).astype(jnp.bfloat16)
        out = dq_own if t < 2 else dq_partner
        rows = slice((t % 2) * TILE, (t % 2 + 1) * TILE)
        for j in range(GROUP):
            out[rows, j * TILE : (j + 1) * TILE] = dq[j * TILE : (j + 1) * TILE, :]
    for b, out in enumerate((out0, out1, out2, out3)):
        rows = slice(b * half, (b + 1) * half)
        out[0:half, :] = dk_acc[rows, :].astype(out.dtype)
        out[half : 2 * half, :] = dv_acc[rows, :].astype(out.dtype)


def head_backward(ids, mask, q_own, g_own, qg_partner, blocks):
    vmem = pl.BlockSpec(memory_space=pltpu.VMEM)
    smem = pl.BlockSpec(memory_space=pltpu.SMEM)
    flops = 8 * 10 * 2 * QUERY_TILES * TILE * TILE * WIDE
    return pl.pallas_call(
        kernel,
        out_shape=(
            jax.ShapeDtypeStruct((ROWS, WIDE), jnp.bfloat16),
            jax.ShapeDtypeStruct((ROWS, WIDE), jnp.bfloat16),
            jax.ShapeDtypeStruct((4 * ROWS, HEAD_WIDTH), jnp.float32),
            jax.ShapeDtypeStruct((4 * ROWS, HEAD_WIDTH), jnp.bfloat16),
            jax.ShapeDtypeStruct((4 * ROWS, HEAD_WIDTH), jnp.bfloat16),
            jax.ShapeDtypeStruct((4 * ROWS, HEAD_WIDTH), jnp.bfloat16),
        ),
        in_specs=[smem, smem] + [vmem] * 7,
        out_specs=(vmem,) * 6,
        scratch_shapes=[
            pltpu.VMEM((QUERY_TILES, WIDE, HEAD_WIDTH), jnp.bfloat16),
            pltpu.VMEM((QUERY_TILES, WIDE, HEAD_WIDTH), jnp.bfloat16),
            pltpu.VMEM((KEY_TILES // 2 - 1, 2 * TILE, WIDE), jnp.float32),
            pltpu.VMEM((KEY_TILES // 2 - 1, 2 * TILE, WIDE), jnp.float32),
            pltpu.VMEM((KEY_TILES // 2, 8, WIDE), jnp.float32),
            pltpu.VMEM((QUERY_TILES, 2 * TILE, WIDE), jnp.float32),
            pltpu.VMEM((QUERY_TILES, 2 * TILE, WIDE), jnp.float32),
            pltpu.VMEM((QUERY_TILES, 8, WIDE), jnp.float32),
            pltpu.VMEM((QUERY_TILES, WIDE, HEAD_WIDTH), jnp.float32),
            pltpu.VMEM((KEY_TILES * TILE, HEAD_WIDTH), jnp.float32),
            pltpu.VMEM((KEY_TILES * TILE, HEAD_WIDTH), jnp.float32),
            pltpu.VMEM((KEY_TILES * TILE, HEAD_WIDTH), jnp.bfloat16),
            pltpu.VMEM((KEY_TILES * TILE, HEAD_WIDTH), jnp.bfloat16),
            pltpu.SMEM((QUERY_TILES, KEY_TILES + 4), jnp.int32),
            pltpu.SMEM((QUERY_TILES,), jnp.int32),
        ],
        compiler_params=pltpu.CompilerParams(vmem_limit_bytes=26 * 1024 * 1024),
        cost_estimate=pl.CostEstimate(flops=flops, bytes_accessed=6_000_000, transcendentals=0),
    )(ids, mask, q_own, g_own, qg_partner, *blocks)


def ring_pairs(dy, dx):
    pairs = []
    for c in range(8):
        y, x = divmod(c, 2)
        pairs.append((c, ((y + dy) % 4) * 2 + (x + dx) % 2))
    return pairs


def move(value, dy, dx):
    return lax.ppermute(value, "ctx", ring_pairs(dy, dx))


def local(queries, key_vectors, value_vectors, output_gradient, tree_mask, tile_order):
    x = lax.axis_index("ctx") % 2

    def columns(array, side, head, width):
        return lax.dynamic_slice_in_dim(array, (2 * side + head) * width, width, axis=1)

    both_wide = 2 * HEAD_WIDTH
    ids_row = jnp.pad(tile_order.astype(jnp.bfloat16), (0, both_wide - 2))
    ids_rows = jnp.broadcast_to(ids_row[None, :], (16, both_wide))
    sent = jnp.concatenate(
        [
            lax.dynamic_slice_in_dim(a, (1 - x) * both_wide, both_wide, axis=1)
            for a in (key_vectors, value_vectors)
        ]
        + [ids_rows],
        axis=0,
    )
    got = move(sent, 0, 1)
    both_ids = ids_rows[:, :HEAD_WIDTH] + jnp.roll(got[2 * ROWS :, :HEAD_WIDTH], 2, axis=1)

    partner_qg = [
        move(
            jnp.concatenate(
                [
                    columns(queries, 1 - x, h, WIDE),
                    columns(output_gradient, 1 - x, h, WIDE),
                ],
                axis=0,
            ),
            0,
            1,
        )
        for h in range(2)
    ]
    steps = (1, -1, 2)
    query_own, query_back, home = [], [], []
    ids = None
    for h in range(2):
        mine = jnp.concatenate(
            [
                columns(key_vectors, x, h, HEAD_WIDTH),
                got[0:ROWS, h * HEAD_WIDTH : (h + 1) * HEAD_WIDTH],
                columns(value_vectors, x, h, HEAD_WIDTH),
                got[ROWS : 2 * ROWS, h * HEAD_WIDTH : (h + 1) * HEAD_WIDTH],
                both_ids,
            ],
            axis=0,
        )
        arrived = [move(mine, s, 0) for s in steps]
        if ids is None:
            ids = jnp.concatenate([b[4 * ROWS, 0:4] for b in [mine] + arrived]).astype(jnp.int32)
        outs = head_backward(
            ids,
            tree_mask,
            columns(queries, x, h, WIDE),
            columns(output_gradient, x, h, WIDE),
            partner_qg[h],
            [mine] + arrived,
        )
        if h == 1:
            parts, query_back[0] = lax.optimization_barrier((outs[1:], query_back[0]))
            outs = (outs[0],) + tuple(parts)
        query_own.append(outs[0])
        query_back.append(move(outs[1], 0, 1))
        total = outs[2]
        for i in (2, 1, 0):
            total = total + move(outs[3 + i], -steps[i], 0).astype(jnp.float32)
        away = jnp.concatenate([total[ROWS : 2 * ROWS], total[3 * ROWS : 4 * ROWS]], axis=0)
        back = move(away.astype(jnp.bfloat16), 0, 1).astype(jnp.float32)
        home.append((total[0:ROWS], total[2 * ROWS : 3 * ROWS], back[0:ROWS], back[ROWS:]))
    first = x == 0

    def arrange(own, other):
        low = [jnp.where(first, a, b) for a, b in zip(own, other)]
        high = [jnp.where(first, b, a) for a, b in zip(own, other)]
        return jnp.concatenate(low + high, axis=1)

    query_gradient = arrange(query_own, query_back)
    key_gradient = arrange([h[0] for h in home], [h[2] for h in home]) * INV_ROOT
    value_gradient = arrange([h[1] for h in home], [h[3] for h in home])
    return query_gradient, key_gradient.astype(jnp.bfloat16), value_gradient.astype(jnp.bfloat16)


def solution(mesh):
    placed = (
        P(("dp", "ctx"), None),
        P(("dp", "ctx"), None),
        P(("dp", "ctx"), None),
        P(("dp", "ctx"), None),
        P("dp", None),
        P(("dp", "ctx")),
    )
    return jax.shard_map(
        local,
        mesh=mesh,
        in_specs=placed,
        out_specs=(P(("dp", "ctx"), None), P(("dp", "ctx"), None), P(("dp", "ctx"), None)),
        check_vma=False,
    )
```

```python
import functools

import jax
import jax.numpy as jnp
from jax import lax
from jax.experimental import pallas as pl
from jax.experimental.pallas import tpu as pltpu
from jax.sharding import PartitionSpec as P

QUERY_HEADS = 20
KEY_HEADS = 4
HEAD_WIDTH = 128
TILE = 128
GROUP = 5
LOG2E = 1.4426950408889634
INV_ROOT = HEAD_WIDTH**-0.5
NEG = -1e30
ROWS = 256
KEY_BLOCKS = 4
KEY_TILES = 16
QUERY_TILES = 4
WIDE = GROUP * TILE
NT_DIMS = (((1,), (1,)), ((), ()))
TN_DIMS = (((0,), (0,)), ((), ()))


def dot(a, b):
    return jnp.dot(a, b, preferred_element_type=jnp.float32)


def kernel(
    ids_ref,
    mask_ref,
    q_own,
    g_own,
    qg_partner,
    kv0,
    kv1,
    kv2,
    kv3,
    dq_own,
    dq_partner,
    out0,
    out1,
    out2,
    out3,
    q_all,
    g_all,
    e_all,
    dp_all,
    top_all,
    e_first,
    dp_first,
    stats,
    dq_all,
    dk_acc,
    dv_acc,
    k_all,
    v_all,
    list_ref,
    count_ref,
):
    blocks = (kv0, kv1, kv2, kv3)
    half = 2 * ROWS
    for b in range(KEY_BLOCKS):
        k_all[b * half : (b + 1) * half, :] = blocks[b][0:half, :]
        v_all[b * half : (b + 1) * half, :] = blocks[b][half : 2 * half, :]
    for t in range(QUERY_TILES):
        for j in range(GROUP):
            to = slice(j * TILE, (j + 1) * TILE)
            if t < 2:
                rows = slice(t * TILE, (t + 1) * TILE)
                q_all[t, to, :] = q_own[rows, to]
                g_all[t, to, :] = g_own[rows, to]
            else:
                rows = slice((t - 2) * TILE, (t - 1) * TILE)
                q_all[t, to, :] = qg_partner[rows, to]
                g_all[t, to, :] = qg_partner[slice(ROWS + (t - 2) * TILE, ROWS + (t - 1) * TILE), to]
    key_row = lax.broadcasted_iota(jnp.int32, (TILE, TILE), 0)
    query_col = lax.broadcasted_iota(jnp.int32, (TILE, TILE), 1)
    causal = key_row <= query_col

    evens, counts = [], []
    for t in range(QUERY_TILES):
        my_tile = ids_ref[t]

        def collect(u, count, t=t, my_tile=my_tile):
            list_ref[t, count] = u
            return count + jnp.where(mask_ref[my_tile, ids_ref[u]] == 1, 1, 0)

        ancestors = lax.fori_loop(0, KEY_TILES, collect, 2) - 2
        even = ancestors % 2 == 1
        last = list_ref[t, ancestors + 1]
        list_ref[t, 0] = t
        list_ref[t, 1] = jnp.where(even, last, t)
        chunks = 1 + ancestors // 2
        count_ref[t] = chunks
        evens.append(even)

    def tiles_of(t, c):
        first = pl.multiple_of(list_ref[t, 2 * c] * TILE, TILE)
        second = pl.multiple_of(list_ref[t, 2 * c + 1] * TILE, TILE)
        return first, second

    def rows_of(ref, tiles):
        return jnp.concatenate([ref[pl.ds(i, TILE), :] for i in tiles], axis=0)

    def products(t, c):
        tiles = tiles_of(t, c)
        s = lax.dot_general(rows_of(k_all, tiles), q_all[t], NT_DIMS, preferred_element_type=jnp.float32)
        dp = lax.dot_general(rows_of(v_all, tiles), g_all[t], NT_DIMS, preferred_element_type=jnp.float32)
        return s * (INV_ROOT * LOG2E), dp

    def spread(t, c, e, dp, factor, delta):
        first, second = tiles_of(t, c)
        p = e * factor
        ds = (p * (dp - delta)).astype(jnp.bfloat16)
        p = p.astype(jnp.bfloat16)
        dv = dot(p, g_all[t])
        dk = dot(ds, q_all[t])
        dv_acc[pl.ds(first, TILE), :] += dv[:TILE]
        dk_acc[pl.ds(first, TILE), :] += dk[:TILE]
        dv_acc[pl.ds(second, TILE), :] += dv[TILE:]
        dk_acc[pl.ds(second, TILE), :] += dk[TILE:]
        return ds, rows_of(k_all, (first, second))

    def gather_dq(ds, k):
        return lax.dot_general(ds, k, TN_DIMS, preferred_element_type=jnp.float32)

    for t in range(QUERY_TILES):
        s, dp = products(t, 0)
        for sums in (dk_acc, dv_acc):
            sums[t * half : (t + 1) * half, :] = jnp.zeros((half, HEAD_WIDTH), jnp.float32)
        ok = jnp.concatenate([causal, jnp.broadcast_to(evens[t], (TILE, TILE))], axis=0)
        s = jnp.where(jnp.concatenate([ok] * GROUP, axis=1), s, NEG)
        top = jnp.max(s, axis=0, keepdims=True)
        e = jnp.exp2(s - top)
        e_first[t] = e
        dp_first[t] = dp
        stats[t, 0:1, :] = top
        stats[t, 1:2, :] = jnp.sum(e, axis=0, keepdims=True)
        stats[t, 2:3, :] = jnp.sum(e * dp, axis=0, keepdims=True)

    def per_query_tile(t, _):
        chunks = count_ref[t]

        def forward(c, carry):
            top, mass, weighted = carry
            s, dp = products(t, c)
            new_top = jnp.maximum(top, jnp.max(s, axis=0, keepdims=True))
            e = jnp.exp2(s - new_top)
            e_all[c - 1] = e
            dp_all[c - 1] = dp
            top_all[c - 1, 0:1, :] = new_top
            shrink = jnp.exp2(top - new_top)
            return (
                new_top,
                mass * shrink + jnp.sum(e, axis=0, keepdims=True),
                weighted * shrink + jnp.sum(e * dp, axis=0, keepdims=True),
            )

        top = stats[t, 0:1, :]
        carry = (top, stats[t, 1:2, :], stats[t, 2:3, :])
        def forward_three(i, carry):
            for j in range(3):
                carry = forward(3 * i + 1 + j, carry)
            return carry

        triples = (chunks - 1) // 3
        carry = lax.fori_loop(0, triples, forward_three, carry)
        final, mass, weighted = lax.fori_loop(1 + 3 * triples, chunks, forward, carry)
        inv_mass = 1.0 / mass
        delta = weighted * inv_mass
        stats[t, 3:4, :] = jnp.exp2(top - final) * inv_mass
        stats[t, 4:5, :] = delta
        dq_all[t] = jnp.zeros((WIDE, HEAD_WIDTH), jnp.float32)

        def backward(c):
            factor = jnp.exp2(top_all[c - 1, 0:1, :] - final) * inv_mass
            return spread(t, c, e_all[c - 1], dp_all[c - 1], factor, delta)

        def backward_three(i, _):
            ds, keys = zip(*[backward(3 * i + 1 + j) for j in range(3)])
            dq_all[t] += gather_dq(jnp.concatenate(ds, axis=0), jnp.concatenate(keys, axis=0))
            return 0

        def backward_one(c, _):
            dq_all[t] += gather_dq(*backward(c))
            return 0

        lax.fori_loop(0, triples, backward_three, 0)
        lax.fori_loop(1 + 3 * triples, chunks, backward_one, 0)
        return 0

    lax.fori_loop(0, QUERY_TILES, per_query_tile, 0)
    for t in range(QUERY_TILES):
        dq = dq_all[t] + gather_dq(*spread(t, 0, e_first[t], dp_first[t], stats[t, 3:4, :], stats[t, 4:5, :]))
        dq = (dq * INV_ROOT).astype(jnp.bfloat16)
        out = dq_own if t < 2 else dq_partner
        rows = slice((t % 2) * TILE, (t % 2 + 1) * TILE)
        for j in range(GROUP):
            out[rows, j * TILE : (j + 1) * TILE] = dq[j * TILE : (j + 1) * TILE, :]
    for b, out in enumerate((out0, out1, out2, out3)):
        rows = slice(b * half, (b + 1) * half)
        out[0:half, :] = dk_acc[rows, :].astype(out.dtype)
        out[half : 2 * half, :] = dv_acc[rows, :].astype(out.dtype)


def head_backward(ids, mask, q_own, g_own, qg_partner, blocks):
    vmem = pl.BlockSpec(memory_space=pltpu.VMEM)
    smem = pl.BlockSpec(memory_space=pltpu.SMEM)
    flops = 8 * 10 * 2 * QUERY_TILES * TILE * TILE * WIDE
    return pl.pallas_call(
        kernel,
        out_shape=(
            jax.ShapeDtypeStruct((ROWS, WIDE), jnp.bfloat16),
            jax.ShapeDtypeStruct((ROWS, WIDE), jnp.bfloat16),
            jax.ShapeDtypeStruct((4 * ROWS, HEAD_WIDTH), jnp.float32),
            jax.ShapeDtypeStruct((4 * ROWS, HEAD_WIDTH), jnp.bfloat16),
            jax.ShapeDtypeStruct((4 * ROWS, HEAD_WIDTH), jnp.bfloat16),
            jax.ShapeDtypeStruct((4 * ROWS, HEAD_WIDTH), jnp.bfloat16),
        ),
        in_specs=[smem, smem] + [vmem] * 7,
        out_specs=(vmem,) * 6,
        scratch_shapes=[
            pltpu.VMEM((QUERY_TILES, WIDE, HEAD_WIDTH), jnp.bfloat16),
            pltpu.VMEM((QUERY_TILES, WIDE, HEAD_WIDTH), jnp.bfloat16),
            pltpu.VMEM((KEY_TILES // 2 - 1, 2 * TILE, WIDE), jnp.float32),
            pltpu.VMEM((KEY_TILES // 2 - 1, 2 * TILE, WIDE), jnp.float32),
            pltpu.VMEM((KEY_TILES // 2, 8, WIDE), jnp.float32),
            pltpu.VMEM((QUERY_TILES, 2 * TILE, WIDE), jnp.float32),
            pltpu.VMEM((QUERY_TILES, 2 * TILE, WIDE), jnp.float32),
            pltpu.VMEM((QUERY_TILES, 8, WIDE), jnp.float32),
            pltpu.VMEM((QUERY_TILES, WIDE, HEAD_WIDTH), jnp.float32),
            pltpu.VMEM((KEY_TILES * TILE, HEAD_WIDTH), jnp.float32),
            pltpu.VMEM((KEY_TILES * TILE, HEAD_WIDTH), jnp.float32),
            pltpu.VMEM((KEY_TILES * TILE, HEAD_WIDTH), jnp.bfloat16),
            pltpu.VMEM((KEY_TILES * TILE, HEAD_WIDTH), jnp.bfloat16),
            pltpu.SMEM((QUERY_TILES, KEY_TILES + 4), jnp.int32),
            pltpu.SMEM((QUERY_TILES,), jnp.int32),
        ],
        compiler_params=pltpu.CompilerParams(vmem_limit_bytes=26 * 1024 * 1024),
        cost_estimate=pl.CostEstimate(flops=flops, bytes_accessed=6_000_000, transcendentals=0),
    )(ids, mask, q_own, g_own, qg_partner, *blocks)


def ring_pairs(dy, dx):
    pairs = []
    for c in range(8):
        y, x = divmod(c, 2)
        pairs.append((c, ((y + dy) % 4) * 2 + (x + dx) % 2))
    return pairs


def move(value, dy, dx):
    return lax.ppermute(value, "ctx", ring_pairs(dy, dx))


def local(queries, key_vectors, value_vectors, output_gradient, tree_mask, tile_order):
    x = lax.axis_index("ctx") % 2

    def columns(array, side, head, width):
        return lax.dynamic_slice_in_dim(array, (2 * side + head) * width, width, axis=1)

    both_wide = 2 * HEAD_WIDTH
    ids_row = jnp.pad(tile_order.astype(jnp.bfloat16), (0, both_wide - 2))
    ids_rows = jnp.broadcast_to(ids_row[None, :], (16, both_wide))
    sent = jnp.concatenate(
        [
            lax.dynamic_slice_in_dim(a, (1 - x) * both_wide, both_wide, axis=1)
            for a in (key_vectors, value_vectors)
        ]
        + [ids_rows],
        axis=0,
    )
    got = move(sent, 0, 1)
    both_ids = ids_rows[:, :HEAD_WIDTH] + jnp.roll(got[2 * ROWS :, :HEAD_WIDTH], 2, axis=1)

    partner_qg = [
        move(
            jnp.concatenate(
                [
                    columns(queries, 1 - x, h, WIDE),
                    columns(output_gradient, 1 - x, h, WIDE),
                ],
                axis=0,
            ),
            0,
            1,
        )
        for h in range(2)
    ]
    steps = (1, -1, 2)
    query_own, query_back, home = [], [], []
    ids = None
    for h in range(2):
        mine = jnp.concatenate(
            [
                columns(key_vectors, x, h, HEAD_WIDTH),
                got[0:ROWS, h * HEAD_WIDTH : (h + 1) * HEAD_WIDTH],
                columns(value_vectors, x, h, HEAD_WIDTH),
                got[ROWS : 2 * ROWS, h * HEAD_WIDTH : (h + 1) * HEAD_WIDTH],
                both_ids,
            ],
            axis=0,
        )
        arrived = [move(mine, s, 0) for s in steps]
        if ids is None:
            ids = jnp.concatenate([b[4 * ROWS, 0:4] for b in [mine] + arrived]).astype(jnp.int32)
        outs = head_backward(
            ids,
            tree_mask,
            columns(queries, x, h, WIDE),
            columns(output_gradient, x, h, WIDE),
            partner_qg[h],
            [mine] + arrived,
        )
        if h == 1:
            parts, query_back[0] = lax.optimization_barrier((outs[1:], query_back[0]))
            outs = (outs[0],) + tuple(parts)
        query_own.append(outs[0])
        query_back.append(move(outs[1], 0, 1))
        total = outs[2]
        for i in (2, 1, 0):
            total = total + move(outs[3 + i], -steps[i], 0).astype(jnp.float32)
        away = jnp.concatenate([total[ROWS : 2 * ROWS], total[3 * ROWS : 4 * ROWS]], axis=0)
        back = move(away.astype(jnp.bfloat16), 0, 1).astype(jnp.float32)
        home.append((total[0:ROWS], total[2 * ROWS : 3 * ROWS], back[0:ROWS], back[ROWS:]))
    first = x == 0

    def arrange(own, other):
        low = [jnp.where(first, a, b) for a, b in zip(own, other)]
        high = [jnp.where(first, b, a) for a, b in zip(own, other)]
        return jnp.concatenate(low + high, axis=1)

    query_gradient = arrange(query_own, query_back)
    key_gradient = arrange([h[0] for h in home], [h[2] for h in home]) * INV_ROOT
    value_gradient = arrange([h[1] for h in home], [h[3] for h in home])
    return query_gradient, key_gradient.astype(jnp.bfloat16), value_gradient.astype(jnp.bfloat16)


def solution(mesh):
    placed = (
        P(("dp", "ctx"), None),
        P(("dp", "ctx"), None),
        P(("dp", "ctx"), None),
        P(("dp", "ctx"), None),
        P("dp", None),
        P(("dp", "ctx")),
    )
    return jax.shard_map(
        local,
        mesh=mesh,
        in_specs=placed,
        out_specs=(P(("dp", "ctx"), None), P(("dp", "ctx"), None), P(("dp", "ctx"), None)),
        check_vma=False,
    )
```

```python
import functools

import jax
import jax.numpy as jnp
from jax import lax
from jax.experimental import pallas as pl
from jax.experimental.pallas import tpu as pltpu
from jax.sharding import PartitionSpec as P

QUERY_HEADS = 20
KEY_HEADS = 4
HEAD_WIDTH = 128
TILE = 128
GROUP = 5
LOG2E = 1.4426950408889634
INV_ROOT = HEAD_WIDTH**-0.5
NEG = -1e30
ROWS = 256
KEY_BLOCKS = 4
KEY_TILES = 16
QUERY_TILES = 4
WIDE = GROUP * TILE
NT_DIMS = (((1,), (1,)), ((), ()))
TN_DIMS = (((0,), (0,)), ((), ()))


def dot(a, b):
    return jnp.dot(a, b, preferred_element_type=jnp.float32)


def kernel(
    ids_ref,
    mask_ref,
    q_own,
    g_own,
    qg_partner,
    kv0,
    kv1,
    kv2,
    kv3,
    dq_own,
    dq_partner,
    out0,
    out1,
    out2,
    out3,
    q_all,
    g_all,
    e_all,
    dp_all,
    top_all,
    e_first,
    dp_first,
    stats,
    dq_all,
    dk_acc,
    dv_acc,
    k_all,
    v_all,
    list_ref,
    count_ref,
):
    blocks = (kv0, kv1, kv2, kv3)
    half = 2 * ROWS
    for b in range(KEY_BLOCKS):
        k_all[b * half : (b + 1) * half, :] = blocks[b][0:half, :]
        v_all[b * half : (b + 1) * half, :] = blocks[b][half : 2 * half, :]
    for t in range(QUERY_TILES):
        for j in range(GROUP):
            to = slice(j * TILE, (j + 1) * TILE)
            if t < 2:
                rows = slice(t * TILE, (t + 1) * TILE)
                q_all[t, to, :] = q_own[rows, to]
                g_all[t, to, :] = g_own[rows, to]
            else:
                rows = slice((t - 2) * TILE, (t - 1) * TILE)
                q_all[t, to, :] = qg_partner[rows, to]
                g_all[t, to, :] = qg_partner[slice(ROWS + (t - 2) * TILE, ROWS + (t - 1) * TILE), to]
    key_row = lax.broadcasted_iota(jnp.int32, (TILE, TILE), 0)
    query_col = lax.broadcasted_iota(jnp.int32, (TILE, TILE), 1)
    causal = key_row <= query_col

    evens, counts = [], []
    for t in range(QUERY_TILES):
        my_tile = ids_ref[t]

        def collect(u, count, t=t, my_tile=my_tile):
            list_ref[t, count] = u
            return count + jnp.where(mask_ref[my_tile, ids_ref[u]] == 1, 1, 0)

        ancestors = lax.fori_loop(0, KEY_TILES, collect, 2) - 2
        even = ancestors % 2 == 1
        last = list_ref[t, ancestors + 1]
        list_ref[t, 0] = t
        list_ref[t, 1] = jnp.where(even, last, t)
        chunks = 1 + ancestors // 2
        count_ref[t] = chunks
        evens.append(even)

    def tiles_of(t, c):
        first = pl.multiple_of(list_ref[t, 2 * c] * TILE, TILE)
        second = pl.multiple_of(list_ref[t, 2 * c + 1] * TILE, TILE)
        return first, second

    def rows_of(ref, tiles):
        return jnp.concatenate([ref[pl.ds(i, TILE), :] for i in tiles], axis=0)

    def products(t, c):
        tiles = tiles_of(t, c)
        s = lax.dot_general(rows_of(k_all, tiles), q_all[t], NT_DIMS, preferred_element_type=jnp.float32)
        dp = lax.dot_general(rows_of(v_all, tiles), g_all[t], NT_DIMS, preferred_element_type=jnp.float32)
        return s * (INV_ROOT * LOG2E), dp

    def spread(t, c, e, dp, factor, delta):
        first, second = tiles_of(t, c)
        p = e * factor
        ds = (p * (dp - delta)).astype(jnp.bfloat16)
        p = p.astype(jnp.bfloat16)
        dv = dot(p, g_all[t])
        dk = dot(ds, q_all[t])
        dv_acc[pl.ds(first, TILE), :] += dv[:TILE]
        dk_acc[pl.ds(first, TILE), :] += dk[:TILE]
        dv_acc[pl.ds(second, TILE), :] += dv[TILE:]
        dk_acc[pl.ds(second, TILE), :] += dk[TILE:]
        return ds, rows_of(k_all, (first, second))

    def gather_dq(ds, k):
        return lax.dot_general(ds, k, TN_DIMS, preferred_element_type=jnp.float32)

    for t in range(QUERY_TILES):
        s, dp = products(t, 0)
        for sums in (dk_acc, dv_acc):
            sums[t * half : (t + 1) * half, :] = jnp.zeros((half, HEAD_WIDTH), jnp.float32)
        ok = jnp.concatenate([causal, jnp.broadcast_to(evens[t], (TILE, TILE))], axis=0)
        s = jnp.where(jnp.concatenate([ok] * GROUP, axis=1), s, NEG)
        top = jnp.max(s, axis=0, keepdims=True)
        e = jnp.exp2(s - top)
        e_first[t] = e
        dp_first[t] = dp
        stats[t, 0:1, :] = top
        stats[t, 1:2, :] = jnp.sum(e, axis=0, keepdims=True)
        stats[t, 2:3, :] = jnp.sum(e * dp, axis=0, keepdims=True)

    def per_query_tile(t, _):
        chunks = count_ref[t]

        def forward(c, carry):
            top, mass, weighted = carry
            s, dp = products(t, c)
            new_top = jnp.maximum(top, jnp.max(s, axis=0, keepdims=True))
            e = jnp.exp2(s - new_top)
            e_all[c - 1] = e
            dp_all[c - 1] = dp
            top_all[c - 1, 0:1, :] = new_top
            shrink = jnp.exp2(top - new_top)
            return (
                new_top,
                mass * shrink + jnp.sum(e, axis=0, keepdims=True),
                weighted * shrink + jnp.sum(e * dp, axis=0, keepdims=True),
            )

        top = stats[t, 0:1, :]
        carry = (top, stats[t, 1:2, :], stats[t, 2:3, :])
        def forward_three(i, carry):
            for j in range(3):
                carry = forward(3 * i + 1 + j, carry)
            return carry

        triples = (chunks - 1) // 3
        carry = lax.fori_loop(0, triples, forward_three, carry)
        final, mass, weighted = lax.fori_loop(1 + 3 * triples, chunks, forward, carry)
        inv_mass = 1.0 / mass
        delta = weighted * inv_mass
        stats[t, 3:4, :] = jnp.exp2(top - final) * inv_mass
        stats[t, 4:5, :] = delta
        dq_all[t] = jnp.zeros((WIDE, HEAD_WIDTH), jnp.float32)

        def backward(c):
            factor = jnp.exp2(top_all[c - 1, 0:1, :] - final) * inv_mass
            return spread(t, c, e_all[c - 1], dp_all[c - 1], factor, delta)

        def backward_three(i, _):
            ds, keys = zip(*[backward(3 * i + 1 + j) for j in range(3)])
            dq_all[t] += gather_dq(jnp.concatenate(ds, axis=0), jnp.concatenate(keys, axis=0))
            return 0

        def backward_one(c, _):
            dq_all[t] += gather_dq(*backward(c))
            return 0

        lax.fori_loop(0, triples, backward_three, 0)
        lax.fori_loop(1 + 3 * triples, chunks, backward_one, 0)
        return 0

    lax.fori_loop(0, QUERY_TILES, per_query_tile, 0)
    for t in range(QUERY_TILES):
        dq = dq_all[t] + gather_dq(*spread(t, 0, e_first[t], dp_first[t], stats[t, 3:4, :], stats[t, 4:5, :]))
        dq = (dq * INV_ROOT).astype(jnp.bfloat16)
        out = dq_own if t < 2 else dq_partner
        rows = slice((t % 2) * TILE, (t % 2 + 1) * TILE)
        for j in range(GROUP):
            out[rows, j * TILE : (j + 1) * TILE] = dq[j * TILE : (j + 1) * TILE, :]
    for b, out in enumerate((out0, out1, out2, out3)):
        rows = slice(b * half, (b + 1) * half)
        out[0:half, :] = dk_acc[rows, :].astype(out.dtype)
        out[half : 2 * half, :] = dv_acc[rows, :].astype(out.dtype)


def head_backward(ids, mask, q_own, g_own, qg_partner, blocks):
    vmem = pl.BlockSpec(memory_space=pltpu.VMEM)
    smem = pl.BlockSpec(memory_space=pltpu.SMEM)
    flops = 8 * 10 * 2 * QUERY_TILES * TILE * TILE * WIDE
    return pl.pallas_call(
        kernel,
        out_shape=(
            jax.ShapeDtypeStruct((ROWS, WIDE), jnp.bfloat16),
            jax.ShapeDtypeStruct((ROWS, WIDE), jnp.bfloat16),
            jax.ShapeDtypeStruct((4 * ROWS, HEAD_WIDTH), jnp.float32),
            jax.ShapeDtypeStruct((4 * ROWS, HEAD_WIDTH), jnp.bfloat16),
            jax.ShapeDtypeStruct((4 * ROWS, HEAD_WIDTH), jnp.bfloat16),
            jax.ShapeDtypeStruct((4 * ROWS, HEAD_WIDTH), jnp.bfloat16),
        ),
        in_specs=[smem, smem] + [vmem] * 7,
        out_specs=(vmem,) * 6,
        scratch_shapes=[
            pltpu.VMEM((QUERY_TILES, WIDE, HEAD_WIDTH), jnp.bfloat16),
            pltpu.VMEM((QUERY_TILES, WIDE, HEAD_WIDTH), jnp.bfloat16),
            pltpu.VMEM((KEY_TILES // 2 - 1, 2 * TILE, WIDE), jnp.float32),
            pltpu.VMEM((KEY_TILES // 2 - 1, 2 * TILE, WIDE), jnp.float32),
            pltpu.VMEM((KEY_TILES // 2, 8, WIDE), jnp.float32),
            pltpu.VMEM((QUERY_TILES, 2 * TILE, WIDE), jnp.float32),
            pltpu.VMEM((QUERY_TILES, 2 * TILE, WIDE), jnp.float32),
            pltpu.VMEM((QUERY_TILES, 8, WIDE), jnp.float32),
            pltpu.VMEM((QUERY_TILES, WIDE, HEAD_WIDTH), jnp.float32),
            pltpu.VMEM((KEY_TILES * TILE, HEAD_WIDTH), jnp.float32),
            pltpu.VMEM((KEY_TILES * TILE, HEAD_WIDTH), jnp.float32),
            pltpu.VMEM((KEY_TILES * TILE, HEAD_WIDTH), jnp.bfloat16),
            pltpu.VMEM((KEY_TILES * TILE, HEAD_WIDTH), jnp.bfloat16),
            pltpu.SMEM((QUERY_TILES, KEY_TILES + 4), jnp.int32),
            pltpu.SMEM((QUERY_TILES,), jnp.int32),
        ],
        compiler_params=pltpu.CompilerParams(vmem_limit_bytes=26 * 1024 * 1024),
        cost_estimate=pl.CostEstimate(flops=flops, bytes_accessed=6_000_000, transcendentals=0),
    )(ids, mask, q_own, g_own, qg_partner, *blocks)


def finish_kernel(own0, own1, back0, back1, key_out, value_out):
    first = lax.axis_index("ctx") % 2 == 0
    for h, (own, back) in enumerate(((own0, back0), (own1, back1))):
        low = slice(h * HEAD_WIDTH, (h + 1) * HEAD_WIDTH)
        high = slice((2 + h) * HEAD_WIDTH, (3 + h) * HEAD_WIDTH)
        for i, (out, scale) in enumerate(((key_out, INV_ROOT), (value_out, 1.0))):
            mine = own[2 * i * ROWS : (2 * i + 1) * ROWS, :] * scale
            theirs = back[i * ROWS : (i + 1) * ROWS, :].astype(jnp.float32) * scale
            out[:, low] = jnp.where(first, mine, theirs).astype(jnp.bfloat16)
            out[:, high] = jnp.where(first, theirs, mine).astype(jnp.bfloat16)


def finish(home):
    vmem = pl.BlockSpec(memory_space=pltpu.VMEM)
    return pl.pallas_call(
        finish_kernel,
        out_shape=(jax.ShapeDtypeStruct((ROWS, KEY_HEADS * HEAD_WIDTH), jnp.bfloat16),) * 2,
        in_specs=[vmem] * 4,
        out_specs=(vmem,) * 2,
        compiler_params=pltpu.CompilerParams(vmem_limit_bytes=8 * 1024 * 1024),
        cost_estimate=pl.CostEstimate(flops=0, bytes_accessed=2_000_000, transcendentals=0),
    )(home[0][0], home[1][0], home[0][1], home[1][1])


def ring_pairs(dy, dx):
    pairs = []
    for c in range(8):
        y, x = divmod(c, 2)
        pairs.append((c, ((y + dy) % 4) * 2 + (x + dx) % 2))
    return pairs


def move(value, dy, dx):
    return lax.ppermute(value, "ctx", ring_pairs(dy, dx))


def local(queries, key_vectors, value_vectors, output_gradient, tree_mask, tile_order):
    x = lax.axis_index("ctx") % 2

    def columns(array, side, head, width):
        return lax.dynamic_slice_in_dim(array, (2 * side + head) * width, width, axis=1)

    both_wide = 2 * HEAD_WIDTH
    ids_row = jnp.pad(tile_order.astype(jnp.bfloat16), (0, both_wide - 2))
    ids_rows = jnp.broadcast_to(ids_row[None, :], (16, both_wide))
    sent = jnp.concatenate(
        [
            lax.dynamic_slice_in_dim(a, (1 - x) * both_wide, both_wide, axis=1)
            for a in (key_vectors, value_vectors)
        ]
        + [ids_rows],
        axis=0,
    )
    got = move(sent, 0, 1)
    both_ids = ids_rows[:, :HEAD_WIDTH] + jnp.roll(got[2 * ROWS :, :HEAD_WIDTH], 2, axis=1)

    partner_qg = [
        move(
            jnp.concatenate(
                [
                    columns(queries, 1 - x, h, WIDE),
                    columns(output_gradient, 1 - x, h, WIDE),
                ],
                axis=0,
            ),
            0,
            1,
        )
        for h in range(2)
    ]
    steps = (1, -1, 2)
    query_own, query_back, home = [], [], []
    ids = None
    for h in range(2):
        mine = jnp.concatenate(
            [
                columns(key_vectors, x, h, HEAD_WIDTH),
                got[0:ROWS, h * HEAD_WIDTH : (h + 1) * HEAD_WIDTH],
                columns(value_vectors, x, h, HEAD_WIDTH),
                got[ROWS : 2 * ROWS, h * HEAD_WIDTH : (h + 1) * HEAD_WIDTH],
                both_ids,
            ],
            axis=0,
        )
        arrived = [move(mine, s, 0) for s in steps]
        if ids is None:
            ids = jnp.concatenate([b[4 * ROWS, 0:4] for b in [mine] + arrived]).astype(jnp.int32)
        outs = head_backward(
            ids,
            tree_mask,
            columns(queries, x, h, WIDE),
            columns(output_gradient, x, h, WIDE),
            partner_qg[h],
            [mine] + arrived,
        )
        if h == 1:
            parts, query_back[0] = lax.optimization_barrier((outs[1:], query_back[0]))
            outs = (outs[0],) + tuple(parts)
        query_own.append(outs[0])
        query_back.append(move(outs[1], 0, 1))
        total = outs[2]
        for i in (2, 1, 0):
            total = total + move(outs[3 + i], -steps[i], 0).astype(jnp.float32)
        away = jnp.concatenate([total[ROWS : 2 * ROWS], total[3 * ROWS : 4 * ROWS]], axis=0)
        home.append((total, move(away.astype(jnp.bfloat16), 0, 1)))
    first = x == 0

    def arrange(own, other):
        low = [jnp.where(first, a, b) for a, b in zip(own, other)]
        high = [jnp.where(first, b, a) for a, b in zip(own, other)]
        return jnp.concatenate(low + high, axis=1)

    query_gradient = arrange(query_own, query_back)
    key_gradient, value_gradient = finish(home)
    return query_gradient, key_gradient, value_gradient


def solution(mesh):
    placed = (
        P(("dp", "ctx"), None),
        P(("dp", "ctx"), None),
        P(("dp", "ctx"), None),
        P(("dp", "ctx"), None),
        P("dp", None),
        P(("dp", "ctx")),
    )
    return jax.shard_map(
        local,
        mesh=mesh,
        in_specs=placed,
        out_specs=(P(("dp", "ctx"), None), P(("dp", "ctx"), None), P(("dp", "ctx"), None)),
        check_vma=False,
    )
```
